512 devices in a mesh: seq: 4 (over y), mp: 32 (over z, core), cache: 4 (over x).
Axes of the slice: x: 4, y: 4, z: 16, core: 2. Of those that a mesh axis runs over, the one named last changes fastest.
Arguments:
- queries: bfloat16 [4, 1024, 8192], P('cache', 'seq', 'mp'), may hold values from -7 to 7
- span_kv: bfloat16 [4, 1024, 8, 256], P('cache', 'seq'), may hold values from -4 to 4
- pool_kv: bfloat16 [2048, 16, 8, 256], P(('mp', 'cache')), may hold values from -4 to 4
- page_owner: int32 [4, 416, 1], replicated, may hold values from 0 to 127; in each aligned block of 104 rows (0 to 103, 104 to 207, ..., all dimensions but the last counted through in order) at most 2 rows name the same one
- page_slot: int32 [4, 416], replicated, may hold values from 0 to 15
- prefix_len: int32 [4], replicated, may hold values from 1 to 6656, 16640 in all
- ssm_input: bfloat16 [4, 1024, 16384], P('cache', 'seq', 'mp'), may hold values from -6 to 6
- gate_z: bfloat16 [4, 1024, 16384], P('cache', 'seq', 'mp'), may hold values from -6 to 6
- time_step: float32 [4, 1024, 16384], P('cache', 'seq', 'mp'), may hold values from 0 to 0.5, as said below
- bc_weight: bfloat16 [16384, 32], P('mp'), may hold values from -0.046875 to 0.046875
- decay_rate: float32 [16384, 16], P('mp'), may hold values from 0.5 to 2
- skip_gain: float32 [16384], P('mp'), may hold values from 0.5 to 1.5
- state_pool: float32 [16, 16384, 16], P('cache', 'mp'), may hold values from -5 to 5
- state_owner: int32 [4], replicated, may hold values from 0 to 3
- state_slot: int32 [4], replicated, may hold values from 0 to 3
Outputs:
- attn_out: float32 [4, 1024, 8192], P('cache', 'seq', 'mp')
- ssm_out: float32 [4, 1024, 16384], P('cache', 'seq', 'mp')
The draws below stay inside these ranges and needn't reach their ends.
Inputs may be any that keep to these rules, and one draw needn't show every extreme that they name: `page_owner`: owners are numbered mp index * 4 + cache index. Among the 104 pages of one request and one sequence group (aligned blocks of rows) no owner appears more than 2 times. `time_step`: Positive.
All inputs are finite; a program needn't handle non-finite values.
Results may differ from the reference program's by a relative error of at most 0.0055.
Values may be sent and summed in bfloat16 or wider, within the bound.
No kernel may reach another device: no remote copies, remote signals or barrier semaphores. Data moves between devices by JAX's collectives and lax.ppermute only.
A program may use at most 64 MiB of HBM per device.

```python
import math
import jax
import jax.numpy as jnp
import numpy as np
from jax import lax

HEADS = 64
KVH = 8
HD = 128
DI = 16384
NS = 16
PAGE = 16
TOK_DEV = 256
PREF_DEV = 104
POOL_DEV = 16
STATE_DEV = 4
NUM_DEMANDS = 4
WINDOW_EXTENT = 1024
PREF_PAGES = 416
PREF_TOK = 6656
OWNERS = 128
CAP = 2
N_CACHE = 4


def draw_queries(key, part):
    key = jax.random.fold_in(key, 11)
    payload_vectors = jnp.clip(jax.random.normal(key, (NUM_DEMANDS, WINDOW_EXTENT, HEADS * HD), jnp.float32), -4.0, 4.0)
    return payload_vectors.astype(jnp.bfloat16)


def draw_span_kv(key, part):
    key = jax.random.fold_in(key, 12)
    payload_vectors = jnp.clip(jax.random.normal(key, (NUM_DEMANDS, WINDOW_EXTENT, KVH, 2 * HD), jnp.float32), -4.0, 4.0)
    return payload_vectors.astype(jnp.bfloat16)


def draw_time_step(key, part):
    key = jax.random.fold_in(key, 13)
    derived_seeds = jax.random.split(key, 4)
    fast_share = 0.5
    is_fast = jax.random.uniform(derived_seeds[0], (1, 1, DI), jnp.float32) < fast_share
    nominal_frequency = jnp.where(is_fast, 0.025, 0.5 / WINDOW_EXTENT)
    rough_scaling = jax.random.uniform(derived_seeds[1], (NUM_DEMANDS, WINDOW_EXTENT, DI), jnp.float32, 0.5, 1.5)
    block_draw = jax.random.uniform(derived_seeds[2], (NUM_DEMANDS, WINDOW_EXTENT // TOK_DEV, 1, DI), jnp.float32)
    segment_scaling = jnp.exp2(2.0 * block_draw - 1.0)
    segment_scaling = jnp.broadcast_to(segment_scaling, (NUM_DEMANDS, WINDOW_EXTENT // TOK_DEV, TOK_DEV, DI)).reshape(NUM_DEMANDS, WINDOW_EXTENT, DI)
    surge_offset = jax.random.randint(derived_seeds[3], (NUM_DEMANDS, 3), 0, WINDOW_EXTENT)
    surge_markers = jnp.any(jnp.arange(WINDOW_EXTENT)[None, :, None] == surge_offset[:, None, :], axis=-1)
    payload_vectors = nominal_frequency * rough_scaling * segment_scaling + jnp.where(surge_markers[:, :, None], 0.35, 0.0)
    return payload_vectors.astype(jnp.float32)


def touch_ends(values, stream_key, low, largest):
    longest = values.shape.index(max(values.shape))
    spots = []
    for shift in (0, 1):
        where = [jax.random.randint(jax.random.fold_in(stream_key, axis), (), 0, length) for axis, length in enumerate(values.shape)]
        where[longest] = (where[longest] + shift) % values.shape[longest]
        spots.append(tuple(where))
    return values.at[spots[0]].set(low).at[spots[1]].set(largest)


def level_of(own_key, extent, shards, low, largest):
    level = 1.0
    for axis_at, shards_of in shards:
        draws = jax.random.uniform(jax.random.fold_in(jax.random.fold_in(own_key, 6), axis_at), (shards_of,), jnp.float32, low / len(shards), largest / len(shards))
        level = level * jnp.repeat(jnp.exp(draws), extent[axis_at] // shards_of).reshape((-1,) + (1,) * (len(extent) - 1 - axis_at))
    return level


def length_profile(count, total, most, slope):
    weights = [(1 << 20) // math.isqrt(rank ** slope) + 1 for rank in range(2, count + 1)]
    surplus, given = total - most - (count - 1), [1] * (count - 1)
    while surplus > 0:
        candidates = [i for i in range(count - 1) if given[i] < most]
        pool, left = sum([weights[i] for i in candidates]), surplus
        for i in candidates:
            more = min(most - given[i], max(1, left * weights[i] // pool), surplus)
            given[i] = given[i] + more
            surplus = surplus - more
    return np.array([most] + given)


def ragged_sizes(rng, count, total, most, slope):
    if count == 2:
        one = jax.random.randint(rng, (), max(1, total - most), min(most, total - 1) + 1)
        return jnp.stack([one, total - one])
    tallies = jnp.asarray(length_profile(count, total, most, slope), jnp.int32)
    couples = (count - 1) // 2
    donor, sink = tallies[1:1 + 2 * couples:2], tallies[2:2 + 2 * couples:2]
    slack = jnp.minimum(donor - 1, most - sink)
    shifted = jax.random.randint(jax.random.fold_in(rng, 1), (couples,), 0, 1 << 20) % (slack + 1)
    tallies = tallies.at[1:1 + 2 * couples:2].set(donor - shifted).at[2:2 + 2 * couples:2].set(sink + shifted)
    return tallies[jax.random.permutation(jax.random.fold_in(rng, 2), count)]


def routed_block(stream_key, own, number, rows, count, top, most, skew):
    sequence = jax.random.permutation(stream_key, count)
    packed, ordinary = portions_of(count, rows * top, most, skew, True), portions_of(count, rows * top, most, skew, False)
    places = jnp.arange(count)

    def named(lengths, rotation):
        used = int((lengths > 0).sum())
        fixed = max(1, used // 4)
        shifted = fixed + (places - fixed + rotation * (used - fixed)) % max(1, count - fixed)
        return jnp.zeros((count,), jnp.int32).at[sequence[jnp.where(places < fixed, places, shifted)]].set(jnp.asarray(lengths, jnp.int32))

    lengths = jnp.where(number % 4 == 0, named(packed, number // 4), named(ordinary, number - number // 4 - 1))
    mixed = jax.random.permutation(jax.random.fold_in(own, 3), count)
    source_of, taker = mixed[0:count // 2 * 2:2], mixed[1:count // 2 * 2:2]
    room = jnp.minimum(lengths[source_of] - 1, most - lengths[taker]) // 2
    room = jnp.where((source_of == sequence[0]) | (taker == sequence[0]) | (lengths[taker] == 0), 0, jnp.maximum(room, 0))
    shifted = jax.random.randint(jax.random.fold_in(own, 4), (count // 2,), 0, 1 << 20) % (room + 1)
    lengths = lengths.at[source_of].add(-shifted).at[taker].add(shifted)
    members = jnp.searchsorted(jnp.cumsum(lengths), jnp.arange(rows * top), side="right").astype(jnp.int32)
    table = members.reshape(top, rows).T
    table = table[jax.random.permutation(jax.random.fold_in(own, 1), rows)]
    rotation = jax.random.randint(jax.random.fold_in(own, 2), (rows, 1), 0, top)
    return jnp.take_along_axis(table, (jnp.arange(top)[None, :] + rotation) % top, axis=1)


def portions_of(number_of, total, reach, slope, full):
    weights = [(1 << 20) // math.isqrt(grade ** slope) + 1 for grade in range(1, number_of + 1)]
    largest = reach if full else min(reach, max(-(-total // number_of), total * weights[0] // sum(weights)))
    least = 1 if total - largest >= number_of - 1 else 0
    counts, surplus = [largest] + [least] * (number_of - 1), total - largest - least * (number_of - 1)
    while surplus > 0:
        candidates = [i for i in range(1, number_of) if counts[i] < largest] or [i for i in range(1, number_of) if counts[i] < reach]
        pool, remaining = sum([weights[i] for i in candidates]), surplus
        for i in candidates:
            addition = min(reach - counts[i], max(1, remaining * weights[i] // pool), surplus)
            counts[i] = counts[i] + addition
            surplus = surplus - addition
    return np.array(counts)


def centred(key, extent, scale, most, cuts=(), kind=jnp.bfloat16):
    entries = scale * jax.random.normal(key, extent, jnp.float32)
    if cuts:
        entries = entries * level_of(key, extent, cuts, -0.22, 0.18)
    return jnp.clip(entries, -most, most).astype(kind)


def setup_inputs(seed: int = 0) -> dict:
    keys = jax.random.split(jax.random.key(seed), 16)
    queries = draw_queries(jax.random.fold_in(keys[15], 71), 0)
    span_kv = draw_span_kv(jax.random.fold_in(keys[15], 71), 0)
    pool_kv = centred(keys[2], (OWNERS * POOL_DEV, PAGE, KVH, 2 * HD), 1.0, 4.0, ((0, 128),))
    page_owner_keys = jax.random.split(jax.random.fold_in(keys[3], 1), NUM_DEMANDS * PREF_PAGES // PREF_DEV)
    page_owner_turns = jax.random.permutation(jax.random.fold_in(keys[3], 3), NUM_DEMANDS * PREF_PAGES // PREF_DEV)
    page_owner = jax.vmap(lambda own, number: routed_block(jax.random.fold_in(keys[3], 2), own, number, PREF_DEV, OWNERS, 1, CAP, 2))(page_owner_keys, page_owner_turns).reshape((NUM_DEMANDS, PREF_PAGES, 1))
    page_slot = touch_ends(jax.random.randint(keys[4], (NUM_DEMANDS, PREF_PAGES), 0, POOL_DEV), jax.random.fold_in(keys[4], 1), 0, POOL_DEV - 1).astype(jnp.int32)
    prefix_len = ragged_sizes(keys[5], NUM_DEMANDS, 5 * PREF_TOK // 2, PREF_TOK, 2).astype(jnp.int32)
    ssm_input = centred(keys[6], (NUM_DEMANDS, WINDOW_EXTENT, DI), 1.0, 6.0, ((0, 4), (1, 4), (2, 32)))
    gate_z = centred(keys[7], (NUM_DEMANDS, WINDOW_EXTENT, DI), 1.0, 6.0, ((0, 4), (1, 4), (2, 32)))
    time_step = draw_time_step(jax.random.fold_in(keys[15], 71), 0)
    bc_weight = centred(keys[9], (DI, 2 * NS), DI ** -0.5, 0.046875, ((0, 32),))
    decay_rate = jnp.clip(jnp.exp(math.log(2.0) - 1.3862944 * jax.random.uniform(keys[10], (DI, NS), jnp.float32) ** level_of(keys[10], (DI, NS), ((0, 32),), -0.2, 0.2)), 0.5, 2.0)
    skip_gain = jnp.clip(0.5 + 1.0 * jax.random.uniform(keys[11], (DI,), jnp.float32) ** level_of(keys[11], (DI,), ((0, 32),), -0.2, 0.2), 0.5, 1.5)
    state_pool = centred(keys[12], (N_CACHE * STATE_DEV, DI, NS), 1.0, 5.0, ((0, 4), (1, 32)), jnp.float32)
    state_owner = touch_ends(jax.random.randint(keys[13], (NUM_DEMANDS,), 0, N_CACHE), jax.random.fold_in(keys[13], 1), 0, N_CACHE - 1).astype(jnp.int32)
    state_slot = touch_ends(jax.random.randint(keys[14], (NUM_DEMANDS,), 0, STATE_DEV), jax.random.fold_in(keys[14], 1), 0, STATE_DEV - 1).astype(jnp.int32)
    return {"queries": queries, "span_kv": span_kv, "pool_kv": pool_kv, "page_owner": page_owner, "page_slot": page_slot, "prefix_len": prefix_len, "ssm_input": ssm_input, "gate_z": gate_z, "time_step": time_step, "bc_weight": bc_weight, "decay_rate": decay_rate, "skip_gain": skip_gain, "state_pool": state_pool, "state_owner": state_owner, "state_slot": state_slot}


big_pos = 1 << 30

def reference(queries, span_kv, pool_kv, page_owner, page_slot, prefix_len, ssm_input, gate_z, time_step, bc_weight, decay_rate, skip_gain, state_pool, state_owner, state_slot):
    head_group = HEADS // KVH
    score_scale = 1.0 / math.sqrt(HD)
    query_rows = math.gcd(WINDOW_EXTENT, 256)

    def one_request(request):
        pool_rows = page_owner[request, :, 0] * POOL_DEV + page_slot[request]
        prefix = pool_kv[pool_rows].reshape(PREF_TOK, KVH, 2 * HD)
        prefix_index = jnp.arange(PREF_TOK, dtype=jnp.int32)
        prefix_pos = jnp.where(prefix_index < prefix_len[request], -1, big_pos).astype(jnp.int32)
        all_keys = jnp.concatenate([prefix, span_kv[request]], axis=0)
        key_pos = jnp.concatenate([prefix_pos, jnp.arange(WINDOW_EXTENT, dtype=jnp.int32)], axis=0)
        query_blocks = queries[request].reshape(WINDOW_EXTENT // query_rows, query_rows, KVH, head_group, HD)
        query_pos = jnp.arange(WINDOW_EXTENT, dtype=jnp.int32).reshape(WINDOW_EXTENT // query_rows, query_rows)

        def per_block(pieces):
            query_block, block_pos = pieces
            allowed = key_pos[None, :] <= block_pos[:, None]

            def per_head(head_id):
                query_part = lax.dynamic_index_in_dim(query_block, head_id, 1, keepdims=False).astype(jnp.float32)
                head_keys = lax.dynamic_index_in_dim(all_keys, head_id, 1, keepdims=False).astype(jnp.float32)
                scores = jnp.einsum('tgd,nd->gtn', query_part, head_keys[:, :HD]) * score_scale
                scores = jnp.where(allowed[None], scores, -1e+30)
                row_max = lax.optimization_barrier(jnp.max(scores, axis=-1))
                weights = jnp.where(allowed[None], jnp.exp(scores - row_max[..., None]), 0.0)
                rounded = lax.optimization_barrier(weights.astype(jnp.bfloat16))
                mixed = jnp.einsum('gtn,nd->gtd', rounded.astype(jnp.float32), head_keys[:, HD:])
                return mixed / lax.optimization_barrier(jnp.sum(weights, axis=-1))[..., None]
            outputs = lax.map(per_head, jnp.arange(KVH, dtype=jnp.int32))
            return outputs.transpose(2, 0, 1, 3).reshape(query_rows, HEADS * HD)
        result = lax.map(per_block, (query_blocks, query_pos))
        return result.reshape(WINDOW_EXTENT, HEADS * HD).astype(jnp.float32)
    attn_out = lax.map(one_request, jnp.arange(NUM_DEMANDS, dtype=jnp.int32))

    def one_state(request):
        inputs = ssm_input[request].astype(jnp.float32)
        bc_total = jnp.dot(ssm_input[request], bc_weight, preferred_element_type=jnp.float32)
        start_state = state_pool[state_owner[request] * STATE_DEV + state_slot[request]]

        def advance(carried, slices):
            step_now, input_now, b_now, c_now = slices
            carried = jnp.exp(-step_now[:, None] * decay_rate) * carried + (step_now * input_now)[:, None] * b_now[None, :]
            return (carried, lax.optimization_barrier(jnp.sum(carried * c_now[None, :], axis=1)))
        _, read_out = lax.scan(advance, start_state, (time_step[request], inputs, bc_total[:, :NS], bc_total[:, NS:]))
        read_out = read_out + skip_gain[None, :] * inputs
        return (read_out * jax.nn.silu(gate_z[request].astype(jnp.float32))).astype(jnp.float32)
    ssm_out = lax.map(one_state, jnp.arange(NUM_DEMANDS, dtype=jnp.int32))
    return (attn_out, ssm_out)
```

```python
import functools
import math

import jax
import jax.numpy as jnp
from jax import lax
from jax.experimental import pallas as pl
from jax.experimental.pallas import tpu as pltpu
from jax.sharding import PartitionSpec as P

LOG2E = math.log2(math.e)
HIDDEN = -1e30
FLOOR = -1e29
LANES = 128
STAT_ROWS = 16
MIB = 1 << 20


def params(mib):
    return pltpu.CompilerParams(vmem_limit_bytes=mib * MIB)


def smem():
    return pl.BlockSpec(memory_space=pltpu.SMEM)


def vmem():
    return pl.BlockSpec(memory_space=pltpu.VMEM)


def pack_kernel(chosen_ref, pool_ref, out_ref):
    rows = lax.broadcasted_iota(jnp.int32, (256, 256), 0)
    columns = lax.broadcasted_iota(jnp.int32, (256, 256), 1)
    token, slot, part, head = rows & 3, (rows >> 2) & 1, (rows >> 3) & 3, rows >> 5
    wanted = slot * 128 + (part * 4 + token) * 8 + head
    pick = (columns == wanted).astype(jnp.float32).astype(jnp.bfloat16)
    for request in range(out_ref.shape[0]):
        pages = jnp.concatenate(
            [pool_ref[chosen_ref[2 * request]], pool_ref[chosen_ref[2 * request + 1]]], axis=0
        )
        out_ref[request] = jnp.dot(pick, pages, preferred_element_type=jnp.float32).astype(
            jnp.bfloat16
        )


def compact_kernel(target_ref, received_ref, out_ref):
    count, width = out_ref.shape[0], received_ref.shape[0]
    columns = lax.broadcasted_iota(jnp.int32, (count, width), 1)
    pick = (columns == target_ref[...]).astype(jnp.float32).astype(jnp.bfloat16)
    out_ref[...] = jnp.dot(pick, received_ref[...], preferred_element_type=jnp.float32).astype(
        jnp.bfloat16
    )


def attention_kernel(
    info_ref, query_ref, piece0, piece1, piece2, piece3, span_ref, pos_ref, out_ref, kv_ref
):
    part_rows = piece0.shape[0]
    prefix_rows = 4 * part_rows
    tok_rows = span_ref.shape[0]
    for at, piece in enumerate((piece0, piece1, piece2, piece3)):
        kv_ref[at * part_rows : (at + 1) * part_rows, :] = piece[...]
    kv_ref[prefix_rows:, :] = span_ref[...]
    seq_index, limit = info_ref[0], info_ref[1]
    bias = jnp.where(pos_ref[...] < limit, 0.0, HIDDEN).astype(jnp.float32)
    scale = LOG2E / math.sqrt(LANES)
    row = lax.broadcasted_iota(jnp.int32, (tok_rows, tok_rows), 0)
    column = lax.broadcasted_iota(jnp.int32, (tok_rows, tok_rows), 1)
    stat_row = lax.broadcasted_iota(jnp.int32, (STAT_ROWS, tok_rows), 0)
    for group in range(query_ref.shape[0]):
        seen = row - column + (group - seq_index) * tok_rows >= 0
        stats = jnp.zeros((STAT_ROWS, tok_rows), jnp.float32)
        for head in range(2):
            lanes = slice(head * LANES, (head + 1) * LANES)
            query = query_ref[group, :, lanes]
            dims = (((1,), (1,)), ((), ()))
            far = lax.dot_general(
                query, kv_ref[:prefix_rows, :LANES], dims, preferred_element_type=jnp.float32
            )
            near = lax.dot_general(
                query, kv_ref[prefix_rows:, :LANES], dims, preferred_element_type=jnp.float32
            )
            far = far * scale + bias
            near = jnp.where(seen, near * scale, HIDDEN)
            top = jnp.maximum(
                jnp.max(far, axis=1, keepdims=True), jnp.max(near, axis=1, keepdims=True)
            )
            top = jnp.maximum(top, FLOOR)
            far = jnp.exp2(far - top)
            near = jnp.exp2(near - top)
            total = jnp.sum(far, axis=1, keepdims=True) + jnp.sum(near, axis=1, keepdims=True)
            total = jnp.maximum(total, 1e-37)
            mixed = jnp.dot(
                far.astype(jnp.bfloat16),
                kv_ref[:prefix_rows, LANES:],
                preferred_element_type=jnp.float32,
            ) + jnp.dot(
                near.astype(jnp.bfloat16),
                kv_ref[prefix_rows:, LANES:],
                preferred_element_type=jnp.float32,
            )
            out_ref[group, :tok_rows, lanes] = (mixed / total).astype(jnp.bfloat16)
            level = top + jnp.log2(total)
            level = jnp.transpose(jnp.broadcast_to(level, (tok_rows, LANES)))[:STAT_ROWS]
            high = level.astype(jnp.bfloat16).astype(jnp.float32)
            middle = (level - high).astype(jnp.bfloat16).astype(jnp.float32)
            low = level - high - middle
            for at, value in enumerate((high, middle, low)):
                stats = jnp.where(stat_row == 3 * head + at, value, stats)
        out_ref[group, tok_rows:, :] = stats.astype(jnp.bfloat16)


def combine_kernel(part_ref, out_ref):
    groups = part_ref.shape[0]
    tok_rows = out_ref.shape[0]
    stats = [part_ref[group, tok_rows:, :].astype(jnp.float32) for group in range(groups)]
    shares = []
    for head in range(2):
        levels = [
            stat[3 * head : 3 * head + 1]
            + stat[3 * head + 1 : 3 * head + 2]
            + stat[3 * head + 2 : 3 * head + 3]
            for stat in stats
        ]
        top = functools.reduce(jnp.maximum, levels)
        weights = [jnp.exp2(level - top) for level in levels]
        total = functools.reduce(jnp.add, weights)
        shares.append([weight / total for weight in weights])
    share_row = lax.broadcasted_iota(jnp.int32, (LANES, tok_rows), 0)
    table = jnp.zeros((LANES, tok_rows), jnp.float32)
    for head in range(2):
        for group in range(groups):
            table = jnp.where(share_row == head * groups + group, shares[head][group], table)
    table = jnp.transpose(table)
    for head in range(2):
        lanes = slice(head * LANES, (head + 1) * LANES)
        mixed = jnp.zeros((tok_rows, LANES), jnp.float32)
        for group in range(groups):
            at = head * groups + group
            mixed = mixed + table[:, at : at + 1] * part_ref[group, :tok_rows, lanes].astype(
                jnp.float32
            )
        out_ref[:, lanes] = mixed


BLOCK = 16


def scan_tokens(step_ref, input_ref, bc_ref, decay, state, read_out):
    tokens = step_ref.shape[0]
    n_state = decay.shape[0]

    for half in range(tokens // LANES):
        bc_half = bc_ref[:, half * LANES : (half + 1) * LANES]

        def block(at, carried, half=half, bc_half=bc_half):
            start = pl.multiple_of(half * LANES + at * BLOCK, BLOCK)
            steps = step_ref[pl.ds(start, BLOCK), :]
            inputs = input_ref[pl.ds(start, BLOCK), :].astype(jnp.float32)
            drive = steps * inputs
            turned = pltpu.roll(bc_half, LANES - at * BLOCK, 1)
            rows = []
            for i in range(BLOCK):
                factor = jnp.exp2(steps[i : i + 1] * decay)
                carried = factor * carried + drive[i : i + 1] * turned[:n_state, i : i + 1]
                if read_out is not None:
                    term = carried * turned[n_state:, i : i + 1]
                    rows.append(jnp.sum(term, axis=0, keepdims=True))
            if read_out is not None:
                read_out(start, inputs, jnp.concatenate(rows, axis=0))
            return carried

        state = lax.fori_loop(0, LANES // BLOCK, block, state)
    return state


def local_scan_kernel(step_ref, input_ref, bc_ref, rate_ref, out_ref):
    decay = rate_ref[...] * (-LOG2E)
    n_state = decay.shape[0]
    out_ref[:n_state] = scan_tokens(
        step_ref, input_ref, bc_ref, decay, jnp.zeros(decay.shape, jnp.float32), None
    )
    total = jnp.sum(step_ref[...], axis=0, keepdims=True)
    out_ref[n_state:] = jnp.broadcast_to(total, (out_ref.shape[0] - n_state, total.shape[1]))


def full_scan_kernel(
    info_ref, step_ref, input_ref, gate_ref, bc_ref, rate_ref, skip_ref, carry_ref, start_ref, out_ref
):
    decay = rate_ref[...] * (-LOG2E)
    n_state = decay.shape[0]
    state = start_ref[...]
    for group in range(carry_ref.shape[0] - 1):
        factor = jnp.exp2(carry_ref[group, n_state : n_state + 1, :] * decay)
        moved = factor * state + carry_ref[group, :n_state, :]
        state = jnp.where(group < info_ref[0], moved, state)
    skip = skip_ref[...]

    def read_out(start, inputs, values):
        gate = gate_ref[pl.ds(start, BLOCK), :].astype(jnp.float32)
        out_ref[pl.ds(start, BLOCK), :] = (values + skip * inputs) * (gate / (1.0 + jnp.exp(-gate)))

    scan_tokens(step_ref, input_ref, bc_ref, decay, state, read_out)


def call(kernel, out, specs, args, mib, scratch=()):
    return pl.pallas_call(
        kernel,
        out_shape=out,
        in_specs=specs,
        out_specs=vmem(),
        scratch_shapes=list(scratch),
        compiler_params=params(mib),
    )(*args)


def shared_with(value, axis, groups=None):
    count = len(groups[0]) if groups else lax.axis_size(axis)
    everything = jnp.broadcast_to(value[None], (count,) + value.shape)
    return lax.all_to_all(
        everything, axis, split_axis=0, concat_axis=0, tiled=True, axis_index_groups=groups
    )


def swapped(value, flip):
    count = lax.axis_size("mp")
    return lax.ppermute(value, "mp", [(source, source ^ flip) for source in range(count)])


def on_device(
    queries,
    span_kv,
    pool_kv,
    page_owner,
    page_slot,
    prefix_len,
    ssm_input,
    gate_z,
    time_step,
    bc_weight,
    decay_rate,
    skip_gain,
    state_pool,
    state_owner,
    state_slot,
):
    n_seq, n_mp, n_cache = (lax.axis_size(axis) for axis in ("seq", "mp", "cache"))
    seq_index, mp_index, request = (lax.axis_index(axis) for axis in ("seq", "mp", "cache"))
    tok_rows = queries.shape[1]
    kv_heads, width = span_kv.shape[2], span_kv.shape[3]
    pool_pages, page_len = pool_kv.shape[:2]
    pages_dev = page_owner.shape[1] // n_seq
    sharers = n_mp // kv_heads
    page_part = page_len // sharers
    head, part = mp_index // sharers, mp_index % sharers

    quarter_owner = lax.dynamic_slice_in_dim(page_owner[:, :, 0], seq_index * pages_dev, pages_dev, 1)
    quarter_slot = lax.dynamic_slice_in_dim(page_slot, seq_index * pages_dev, pages_dev, 1)
    earlier = jnp.tril(jnp.ones((pages_dev, pages_dev), jnp.bool_), -1)
    same = quarter_owner[:, :, None] == quarter_owner[:, None, :]
    rank = jnp.sum((same & earlier).astype(jnp.int32), axis=2)
    mine = quarter_owner == mp_index * n_cache + request
    places = jnp.arange(2, dtype=jnp.int32)
    hit = mine[:, None, :] & (rank[:, None, :] == places[None, :, None])
    chosen = jnp.sum(jnp.where(hit, quarter_slot[:, None, :], 0), axis=2).reshape(-1)

    outgoing = call(
        pack_kernel,
        jax.ShapeDtypeStruct((n_cache, n_mp * 2 * page_part, width), jnp.bfloat16),
        [smem(), vmem()],
        (chosen, pool_kv.reshape(pool_pages, page_len * kv_heads, width)),
        24,
    )
    received = lax.all_to_all(
        outgoing.reshape(n_cache * n_mp, 2 * page_part, width),
        ("cache", "mp"),
        split_axis=0,
        concat_axis=0,
        tiled=True,
    ).reshape(n_cache * n_mp * 2 * page_part, width)

    all_queries = shared_with(queries[0], "seq")

    inputs = ssm_input[0]
    bc = lax.dot_general(
        bc_weight, inputs, (((0,), (1,)), ((), ())), preferred_element_type=jnp.float32
    )
    near = [[base + i for i in range(8)] for base in range(0, n_mp, 8)]
    across = [[base + i for i in range(0, n_mp, 8)] for base in range(8)]
    bc = jnp.sum(shared_with(bc, "mp", near), axis=0)
    bc = jnp.sum(shared_with(bc, "mp", across), axis=0)

    states = state_pool.transpose(0, 2, 1)
    leaving = jnp.where((state_owner == request)[:, None, None], states[state_slot], 0.0)
    arriving = lax.all_to_all(leaving, "cache", split_axis=0, concat_axis=0, tiled=True)
    start_state = lax.dynamic_index_in_dim(arriving, state_owner[request], 0, keepdims=False)

    rate = decay_rate.T
    n_state = rate.shape[0]
    carry = call(
        local_scan_kernel,
        jax.ShapeDtypeStruct((n_state + 8, rate.shape[1]), jnp.float32),
        [vmem()] * 4,
        (time_step[0], inputs, bc, rate),
        24,
    )
    carries = shared_with(carry, "seq")
    ssm_out = call(
        full_scan_kernel,
        jax.ShapeDtypeStruct(inputs.shape, jnp.float32),
        [smem()] + [vmem()] * 8,
        (
            seq_index.reshape(1),
            time_step[0],
            inputs,
            gate_z[0],
            bc,
            rate,
            skip_gain.reshape(1, -1),
            carries,
            start_state,
        ),
        24,
    )

    my_owner = lax.dynamic_index_in_dim(quarter_owner, request, 0, keepdims=False)
    my_rank = lax.dynamic_index_in_dim(rank, request, 0, keepdims=False)
    base = ((my_owner % n_cache) * n_mp + my_owner // n_cache) * (2 * page_part) + my_rank * page_part
    tokens = jnp.arange(page_part, dtype=jnp.int32)
    target = (base[None, :] + tokens[:, None]).reshape(-1, 1)
    page = seq_index * pages_dev + jnp.arange(pages_dev, dtype=jnp.int32)
    in_page = (part ^ jnp.arange(sharers, dtype=jnp.int32))[:, None] * page_part + tokens[None, :]
    position = (page[None, None, :] * page_len + in_page[:, :, None]).reshape(1, -1)

    own = call(
        compact_kernel,
        jax.ShapeDtypeStruct((page_part * pages_dev, width), jnp.bfloat16),
        [vmem()] * 2,
        (target, received),
        24,
    )
    pieces = [own] + [swapped(own, flip) for flip in range(1, sharers)]
    span_tile = lax.dynamic_index_in_dim(span_kv[0], head, 1, keepdims=False)
    partial = call(
        attention_kernel,
        jax.ShapeDtypeStruct((n_seq, tok_rows + STAT_ROWS, queries.shape[2]), jnp.bfloat16),
        [smem()] + [vmem()] * 7,
        (
            jnp.stack([seq_index, prefix_len[request]]).astype(jnp.int32),
            all_queries,
            *pieces,
            span_tile,
            position,
        ),
        40,
        [pltpu.VMEM((sharers * page_part * pages_dev + tok_rows, width), jnp.bfloat16)],
    )
    gathered = lax.all_to_all(partial, "seq", split_axis=0, concat_axis=0, tiled=True)
    attn_out = call(
        combine_kernel,
        jax.ShapeDtypeStruct((tok_rows, queries.shape[2]), jnp.float32),
        [vmem()],
        (gathered,),
        24,
    )
    return (attn_out[None], ssm_out[None])


def solution(mesh):
    in_specs = (
        P("cache", "seq", "mp"),
        P("cache", "seq", None, None),
        P(("mp", "cache"), None, None, None),
        P(),
        P(),
        P(),
        P("cache", "seq", "mp"),
        P("cache", "seq", "mp"),
        P("cache", "seq", "mp"),
        P("mp", None),
        P("mp", None),
        P("mp"),
        P("cache", "mp", None),
        P(),
        P(),
    )
    out_specs = (P("cache", "seq", "mp"), P("cache", "seq", "mp"))
    return jax.shard_map(
        on_device, mesh=mesh, in_specs=in_specs, out_specs=out_specs, check_vma=False
    )
```

```python
import functools
import math

import jax
import jax.numpy as jnp
from jax import lax
from jax.experimental import pallas as pl
from jax.experimental.pallas import tpu as pltpu
from jax.sharding import PartitionSpec as P

LOG2E = math.log2(math.e)
HIDDEN = -1e30
FLOOR = -1e29
LANES = 128
STAT_ROWS = 16
MIB = 1 << 20


def params(mib):
    return pltpu.CompilerParams(vmem_limit_bytes=mib * MIB)


def smem():
    return pl.BlockSpec(memory_space=pltpu.SMEM)


def vmem():
    return pl.BlockSpec(memory_space=pltpu.VMEM)


def pack_kernel(chosen_ref, pool_ref, out_ref):
    rows = lax.broadcasted_iota(jnp.int32, (256, 256), 0)
    columns = lax.broadcasted_iota(jnp.int32, (256, 256), 1)
    token, slot, part, head = rows & 3, (rows >> 2) & 1, (rows >> 3) & 3, rows >> 5
    wanted = slot * 128 + (part * 4 + token) * 8 + head
    pick = (columns == wanted).astype(jnp.float32).astype(jnp.bfloat16)
    for request in range(out_ref.shape[0]):
        pages = jnp.concatenate(
            [pool_ref[chosen_ref[2 * request]], pool_ref[chosen_ref[2 * request + 1]]], axis=0
        )
        out_ref[request] = jnp.dot(pick, pages, preferred_element_type=jnp.float32).astype(
            jnp.bfloat16
        )


def compact_kernel(target_ref, received_ref, out_ref):
    count, width = out_ref.shape[0], received_ref.shape[0]
    columns = lax.broadcasted_iota(jnp.int32, (count, width), 1)
    pick = (columns == target_ref[...]).astype(jnp.float32).astype(jnp.bfloat16)
    out_ref[...] = jnp.dot(pick, received_ref[...], preferred_element_type=jnp.float32).astype(
        jnp.bfloat16
    )


def prepare_kernel(owner_ref, slot_ref, state_ref, span_ref, pair_ref, crossing_ref, near_ref, tile_ref):
    request = lax.axis_index("cache")

    def held(index):
        mine = owner_ref[index] == request
        return jnp.where(mine, state_ref[slot_ref[index]], 0.0)

    pair_ref[0] = held(request ^ 1)
    pair_ref[1] = held(request ^ 3)
    crossing_ref[...] = held(request ^ 2)
    near_ref[...] = held(request)
    tokens, heads = tile_ref.shape[0], span_ref.shape[0] // tile_ref.shape[0]
    head = lax.axis_index("mp") >> 2
    some = 32
    rows = lax.broadcasted_iota(jnp.int32, (some, some * heads), 0)
    columns = lax.broadcasted_iota(jnp.int32, (some, some * heads), 1)
    pick = (columns == rows * heads + head).astype(jnp.float32).astype(jnp.bfloat16)
    for at in range(tokens // some):
        block = span_ref[at * some * heads : (at + 1) * some * heads, :]
        tile_ref[at * some : (at + 1) * some, :] = jnp.dot(
            pick, block, preferred_element_type=jnp.float32
        ).astype(jnp.bfloat16)


def attention_kernel(
    prefix_ref, *refs
):
    *queries, piece0, piece1, piece2, piece3, span_ref, out_ref, kv_ref = refs
    part_rows = piece0.shape[0]
    prefix_rows = 4 * part_rows
    tok_rows = span_ref.shape[0]
    for at, piece in enumerate((piece0, piece1, piece2, piece3)):
        kv_ref[at * part_rows : (at + 1) * part_rows, :] = piece[...]
    kv_ref[prefix_rows:, :] = span_ref[...]
    seq_index, limit = lax.axis_index("seq"), prefix_ref[lax.axis_index("cache")]
    own_part = lax.axis_index("mp") & 3
    pages = part_rows // 4
    place = lax.broadcasted_iota(jnp.int32, (1, prefix_rows), 1)
    piece = sum((place >= at * part_rows).astype(jnp.int32) for at in range(1, 4))
    place = place - piece * part_rows
    token = sum((place >= at * pages).astype(jnp.int32) for at in range(1, 4))
    page = place - token * pages + seq_index * pages
    position = page * 16 + (own_part ^ piece) * 4 + token
    bias = jnp.where(position < limit, 0.0, HIDDEN).astype(jnp.float32)
    scale = LOG2E / math.sqrt(LANES)
    row = lax.broadcasted_iota(jnp.int32, (tok_rows, tok_rows), 0)
    column = lax.broadcasted_iota(jnp.int32, (tok_rows, tok_rows), 1)
    stat_row = lax.broadcasted_iota(jnp.int32, (STAT_ROWS, tok_rows), 0)
    for back, query_ref in enumerate(queries):
        group = (seq_index - back) & 3
        seen = row - column + (group - seq_index) * tok_rows >= 0
        stats = jnp.zeros((STAT_ROWS, tok_rows), jnp.float32)
        for head in range(2):
            lanes = slice(head * LANES, (head + 1) * LANES)
            query = query_ref[:, lanes]
            dims = (((1,), (1,)), ((), ()))
            far = lax.dot_general(
                query, kv_ref[:prefix_rows, :LANES], dims, preferred_element_type=jnp.float32
            )
            near = lax.dot_general(
                query, kv_ref[prefix_rows:, :LANES], dims, preferred_element_type=jnp.float32
            )
            far = far * scale + bias
            near = jnp.where(seen, near * scale, HIDDEN)
            top = jnp.maximum(
                jnp.max(far, axis=1, keepdims=True), jnp.max(near, axis=1, keepdims=True)
            )
            top = jnp.maximum(top, FLOOR)
            far = jnp.exp2(far - top)
            near = jnp.exp2(near - top)
            total = jnp.sum(far, axis=1, keepdims=True) + jnp.sum(near, axis=1, keepdims=True)
            total = jnp.maximum(total, 1e-37)
            mixed = jnp.dot(
                far.astype(jnp.bfloat16),
                kv_ref[:prefix_rows, LANES:],
                preferred_element_type=jnp.float32,
            ) + jnp.dot(
                near.astype(jnp.bfloat16),
                kv_ref[prefix_rows:, LANES:],
                preferred_element_type=jnp.float32,
            )
            out_ref[group, :tok_rows, lanes] = (mixed / total).astype(jnp.bfloat16)
            level = top + jnp.log2(total)
            level = jnp.transpose(jnp.broadcast_to(level, (tok_rows, LANES)))[:STAT_ROWS]
            high = level.astype(jnp.bfloat16).astype(jnp.float32)
            middle = (level - high).astype(jnp.bfloat16).astype(jnp.float32)
            low = level - high - middle
            for at, value in enumerate((high, middle, low)):
                stats = jnp.where(stat_row == 3 * head + at, value, stats)
        out_ref[group, tok_rows:, :] = stats.astype(jnp.bfloat16)


def combine_kernel(part_ref, out_ref):
    groups = part_ref.shape[0]
    tok_rows = out_ref.shape[0]
    stats = [part_ref[group, tok_rows:, :].astype(jnp.float32) for group in range(groups)]
    shares = []
    for head in range(2):
        levels = [
            stat[3 * head : 3 * head + 1]
            + stat[3 * head + 1 : 3 * head + 2]
            + stat[3 * head + 2 : 3 * head + 3]
            for stat in stats
        ]
        top = functools.reduce(jnp.maximum, levels)
        weights = [jnp.exp2(level - top) for level in levels]
        total = functools.reduce(jnp.add, weights)
        shares.append([weight / total for weight in weights])
    share_row = lax.broadcasted_iota(jnp.int32, (LANES, tok_rows), 0)
    table = jnp.zeros((LANES, tok_rows), jnp.float32)
    for head in range(2):
        for group in range(groups):
            table = jnp.where(share_row == head * groups + group, shares[head][group], table)
    table = jnp.transpose(table)
    for head in range(2):
        lanes = slice(head * LANES, (head + 1) * LANES)
        mixed = jnp.zeros((tok_rows, LANES), jnp.float32)
        for group in range(groups):
            at = head * groups + group
            mixed = mixed + table[:, at : at + 1] * part_ref[group, :tok_rows, lanes].astype(
                jnp.float32
            )
        out_ref[:, lanes] = mixed


BLOCK = 16


def scan_tokens(step_ref, input_ref, bc_ref, decay, state, read_out):
    tokens = step_ref.shape[0]
    n_state = decay.shape[0]

    for half in range(tokens // LANES):
        bc_half = bc_ref[:, half * LANES : (half + 1) * LANES]

        def block(at, carried, half=half, bc_half=bc_half):
            start = pl.multiple_of(half * LANES + at * BLOCK, BLOCK)
            steps = step_ref[pl.ds(start, BLOCK), :]
            inputs = input_ref[pl.ds(start, BLOCK), :].astype(jnp.float32)
            drive = steps * inputs
            turned = pltpu.roll(bc_half, LANES - at * BLOCK, 1)
            rows = []
            for i in range(BLOCK):
                factor = jnp.exp2(steps[i : i + 1] * decay)
                carried = factor * carried + drive[i : i + 1] * turned[:n_state, i : i + 1]
                if read_out is not None:
                    term = carried * turned[n_state:, i : i + 1]
                    rows.append(jnp.sum(term, axis=0, keepdims=True))
            if read_out is not None:
                read_out(start, inputs, jnp.concatenate(rows, axis=0))
            return carried

        state = lax.fori_loop(0, LANES // BLOCK, block, state)
    return state


def local_scan_kernel(step_ref, input_ref, bc_ref, rate_ref, out_ref):
    decay = rate_ref[...] * (-LOG2E)
    n_state = decay.shape[0]
    out_ref[:n_state] = scan_tokens(
        step_ref, input_ref, bc_ref, decay, jnp.zeros(decay.shape, jnp.float32), None
    )
    total = jnp.sum(step_ref[...], axis=0, keepdims=True)
    out_ref[n_state:] = jnp.broadcast_to(total, (out_ref.shape[0] - n_state, total.shape[1]))


def full_scan_kernel(
    step_ref, input_ref, gate_ref, bc_ref, rate_ref, skip_ref, start_ref, *rest
):
    *carries, out_ref = rest
    decay = rate_ref[...] * (-LOG2E)
    n_state = decay.shape[0]
    state = start_ref[...]
    for back in range(len(carries), 0, -1):
        carry = carries[back - 1]
        factor = jnp.exp2(carry[n_state : n_state + 1, :] * decay)
        moved = factor * state + carry[:n_state, :]
        state = jnp.where(back <= lax.axis_index("seq"), moved, state)
    skip = skip_ref[...]

    def read_out(start, inputs, values):
        gate = gate_ref[pl.ds(start, BLOCK), :].astype(jnp.float32)
        out_ref[pl.ds(start, BLOCK), :] = (values + skip * inputs) * (gate / (1.0 + jnp.exp(-gate)))

    scan_tokens(step_ref, input_ref, bc_ref, decay, state, read_out)


def call(kernel, out, specs, args, mib, scratch=()):
    return pl.pallas_call(
        kernel,
        out_shape=out,
        in_specs=specs,
        out_specs=vmem(),
        scratch_shapes=list(scratch),
        compiler_params=params(mib),
    )(*args)


def shifted(value, axis, steps):
    count = lax.axis_size(axis)
    return lax.ppermute(value, axis, [(i, (i + steps) % count) for i in range(count)])


def from_all(value, axis):
    return [value] + [shifted(value, axis, steps) for steps in range(1, lax.axis_size(axis))]


def swapped(value, flip):
    count = lax.axis_size("mp")
    return lax.ppermute(value, "mp", [(source, source ^ flip) for source in range(count)])


def on_device(
    queries,
    span_kv,
    pool_kv,
    page_owner,
    page_slot,
    prefix_len,
    ssm_input,
    gate_z,
    time_step,
    bc_weight,
    decay_rate,
    skip_gain,
    state_pool,
    state_owner,
    state_slot,
):
    n_seq, n_mp, n_cache = (lax.axis_size(axis) for axis in ("seq", "mp", "cache"))
    seq_index, mp_index, request = (lax.axis_index(axis) for axis in ("seq", "mp", "cache"))
    tok_rows = queries.shape[1]
    kv_heads, width = span_kv.shape[2], span_kv.shape[3]
    pool_pages, page_len = pool_kv.shape[:2]
    pages_dev = page_owner.shape[1] // n_seq
    sharers = n_mp // kv_heads
    page_part = page_len // sharers

    quarter_owner = lax.dynamic_slice_in_dim(page_owner[:, :, 0], seq_index * pages_dev, pages_dev, 1)
    quarter_slot = lax.dynamic_slice_in_dim(page_slot, seq_index * pages_dev, pages_dev, 1)
    earlier = jnp.tril(jnp.ones((pages_dev, pages_dev), jnp.bool_), -1)
    same = quarter_owner[:, :, None] == quarter_owner[:, None, :]
    rank = jnp.sum((same & earlier).astype(jnp.int32), axis=2)
    mine = quarter_owner == mp_index * n_cache + request
    places = jnp.arange(2, dtype=jnp.int32)
    hit = mine[:, None, :] & (rank[:, None, :] == places[None, :, None])
    chosen = jnp.sum(jnp.where(hit, quarter_slot[:, None, :], 0), axis=2).reshape(-1)

    inputs = ssm_input[0]
    sums = lax.dot_general(
        bc_weight, inputs, (((0,), (1,)), ((), ())), preferred_element_type=jnp.float32
    )
    sums = jnp.broadcast_to(sums.astype(jnp.bfloat16)[None], (n_mp // 2,) + sums.shape)
    sums, pool_kv = lax.optimization_barrier((sums, pool_kv))
    chips = [[2 * chip + core for chip in range(n_mp // 2)] for core in range(2)]
    sums = lax.all_to_all(
        sums, "mp", split_axis=0, concat_axis=0, tiled=True, axis_index_groups=chips
    )
    outgoing = call(
        pack_kernel,
        jax.ShapeDtypeStruct((n_cache, n_mp * 2 * page_part, width), jnp.bfloat16),
        [smem(), vmem()],
        (chosen, pool_kv.reshape(pool_pages, page_len * kv_heads, width)),
        24,
    )

    outgoing, sums, queries, state_pool = lax.optimization_barrier(
        (outgoing, sums, queries, state_pool)
    )
    received = lax.all_to_all(
        outgoing.reshape(n_cache * n_mp, 2 * page_part, width),
        ("cache", "mp"),
        split_axis=0,
        concat_axis=0,
        tiled=True,
    ).reshape(n_cache * n_mp * 2 * page_part, width)
    bc = jnp.sum(sums.astype(jnp.float32), axis=0)
    bc = bc + swapped(bc, 1)

    rate = decay_rate.T
    state_shape = jax.ShapeDtypeStruct(rate.shape, jnp.float32)
    pair, crossing, near_state, span_tile = pl.pallas_call(
        prepare_kernel,
        out_shape=(
            jax.ShapeDtypeStruct((2,) + rate.shape, jnp.float32),
            state_shape,
            state_shape,
            jax.ShapeDtypeStruct((tok_rows, width), jnp.bfloat16),
        ),
        in_specs=[smem(), smem(), vmem(), vmem()],
        out_specs=(vmem(),) * 4,
        compiler_params=params(24),
    )(state_owner, state_slot, state_pool.transpose(0, 2, 1), span_kv.reshape(-1, width))
    pair = lax.ppermute(pair, "cache", [(i, i ^ 1) for i in range(n_cache)])
    crossing = crossing + pair[1]
    near_state = near_state + pair[0]
    all_queries = from_all(queries[0], "seq")
    start_state = near_state + lax.ppermute(crossing, "cache", [(i, i ^ 2) for i in range(n_cache)])

    rate = decay_rate.T
    n_state = rate.shape[0]
    carry = call(
        local_scan_kernel,
        jax.ShapeDtypeStruct((n_state + 8, rate.shape[1]), jnp.float32),
        [vmem()] * 4,
        (time_step[0], inputs, bc, rate),
        24,
    )
    last = shifted(carry, "seq", 1)
    decay = jnp.exp2(carry[n_state : n_state + 1] * (rate * (-LOG2E)))
    both = jnp.concatenate(
        [decay * last[:n_state] + carry[:n_state], last[n_state:] + carry[n_state:]], axis=0
    )
    carries = [last, shifted(jnp.where(seq_index > 0, both, carry), "seq", 2)]
    received, carries, start_state, bc, all_queries, span_tile = lax.optimization_barrier(
        (received, carries, start_state, bc, all_queries, span_tile)
    )
    base = ((quarter_owner % n_cache) * n_mp + quarter_owner // n_cache) * 2 + rank
    asked = jnp.arange(n_cache, dtype=jnp.int32)[:, None] == request
    base = jnp.sum(jnp.where(asked, base, 0), axis=0) * page_part
    tokens = jnp.arange(page_part, dtype=jnp.int32)
    target = (base[None, :] + tokens[:, None]).reshape(-1, 1)
    own = call(
        compact_kernel,
        jax.ShapeDtypeStruct((page_part * pages_dev, width), jnp.bfloat16),
        [vmem()] * 2,
        (target, received),
        24,
    )
    across = swapped(own, 2)
    pieces = [own, swapped(own, 1), across, swapped(across, 1)]
    partial = call(
        attention_kernel,
        jax.ShapeDtypeStruct((n_seq, tok_rows + STAT_ROWS, queries.shape[2]), jnp.bfloat16),
        [smem()] + [vmem()] * 9,
        (prefix_len, *all_queries, *pieces, span_tile),
        40,
        [pltpu.VMEM((sharers * page_part * pages_dev + tok_rows, width), jnp.bfloat16)],
    )
    partial, bc, carries = lax.optimization_barrier((partial, bc, carries))
    ssm_out = call(
        full_scan_kernel,
        jax.ShapeDtypeStruct(inputs.shape, jnp.float32),
        [vmem()] * (7 + len(carries)),
        (
            time_step[0],
            inputs,
            gate_z[0],
            bc,
            rate,
            skip_gain.reshape(1, -1),
            start_state,
            *carries,
        ),
        24,
    )
    gathered = lax.all_to_all(partial, "seq", split_axis=0, concat_axis=0, tiled=True)
    attn_out = call(
        combine_kernel,
        jax.ShapeDtypeStruct((tok_rows, queries.shape[2]), jnp.float32),
        [vmem()],
        (gathered,),
        24,
    )
    return (attn_out[None], ssm_out[None])


def solution(mesh):
    in_specs = (
        P("cache", "seq", "mp"),
        P("cache", "seq", None, None),
        P(("mp", "cache"), None, None, None),
        P(),
        P(),
        P(),
        P("cache", "seq", "mp"),
        P("cache", "seq", "mp"),
        P("cache", "seq", "mp"),
        P("mp", None),
        P("mp", None),
        P("mp"),
        P("cache", "mp", None),
        P(),
        P(),
    )
    out_specs = (P("cache", "seq", "mp"), P("cache", "seq", "mp"))
    return jax.shard_map(
        on_device, mesh=mesh, in_specs=in_specs, out_specs=out_specs, check_vma=False
    )
```

```python
import functools
import math

import jax
import jax.numpy as jnp
from jax import lax
from jax.experimental import pallas as pl
from jax.experimental.pallas import tpu as pltpu
from jax.sharding import PartitionSpec as P

LOG2E = math.log2(math.e)
HIDDEN = -1e30
FLOOR = -1e29
LANES = 128
STAT_ROWS = 16
MIB = 1 << 20


def params(mib):
    return pltpu.CompilerParams(vmem_limit_bytes=mib * MIB)


def smem():
    return pl.BlockSpec(memory_space=pltpu.SMEM)


def vmem():
    return pl.BlockSpec(memory_space=pltpu.VMEM)


def pack_kernel(chosen_ref, pool_ref, out_ref):
    rows = lax.broadcasted_iota(jnp.int32, (256, 256), 0)
    columns = lax.broadcasted_iota(jnp.int32, (256, 256), 1)
    token, slot, part, head = rows & 3, (rows >> 2) & 1, (rows >> 3) & 3, rows >> 5
    wanted = slot * 128 + (part * 4 + token) * 8 + head
    pick = (columns == wanted).astype(jnp.float32).astype(jnp.bfloat16)
    for request in range(out_ref.shape[0]):
        pages = jnp.concatenate(
            [pool_ref[chosen_ref[2 * request]], pool_ref[chosen_ref[2 * request + 1]]], axis=0
        )
        out_ref[request] = jnp.dot(pick, pages, preferred_element_type=jnp.float32).astype(
            jnp.bfloat16
        )


def compact_kernel(target_ref, received_ref, out_ref):
    count, width = out_ref.shape[0], received_ref.shape[0]
    columns = lax.broadcasted_iota(jnp.int32, (count, width), 1)
    pick = (columns == target_ref[...]).astype(jnp.float32).astype(jnp.bfloat16)
    out_ref[...] = jnp.dot(pick, received_ref[...], preferred_element_type=jnp.float32).astype(
        jnp.bfloat16
    )


def prepare_kernel(owner_ref, slot_ref, state_ref, span_ref, pair_ref, crossing_ref, near_ref, tile_ref):
    request = lax.axis_index("cache")

    def held(index):
        mine = owner_ref[index] == request
        return jnp.where(mine, state_ref[slot_ref[index]], 0.0)

    pair_ref[0] = held(request ^ 1)
    pair_ref[1] = held(request ^ 3)
    crossing_ref[...] = held(request ^ 2)
    near_ref[...] = held(request)
    tokens, heads = tile_ref.shape[0], span_ref.shape[0] // tile_ref.shape[0]
    head = lax.axis_index("mp") >> 2
    some = 32
    rows = lax.broadcasted_iota(jnp.int32, (some, some * heads), 0)
    columns = lax.broadcasted_iota(jnp.int32, (some, some * heads), 1)
    pick = (columns == rows * heads + head).astype(jnp.float32).astype(jnp.bfloat16)
    for at in range(tokens // some):
        block = span_ref[at * some * heads : (at + 1) * some * heads, :]
        tile_ref[at * some : (at + 1) * some, :] = jnp.dot(
            pick, block, preferred_element_type=jnp.float32
        ).astype(jnp.bfloat16)


def attention_kernel(
    prefix_ref, *refs
):
    *queries, piece0, piece1, piece2, piece3, span_ref, out_ref, kv_ref = refs
    part_rows = piece0.shape[0]
    prefix_rows = 4 * part_rows
    tok_rows = span_ref.shape[0]
    for at, piece in enumerate((piece0, piece1, piece2, piece3)):
        kv_ref[at * part_rows : (at + 1) * part_rows, :] = piece[...]
    kv_ref[prefix_rows:, :] = span_ref[...]
    seq_index, limit = lax.axis_index("seq"), prefix_ref[lax.axis_index("cache")]
    own_part = lax.axis_index("mp") & 3
    pages = part_rows // 4
    place = lax.broadcasted_iota(jnp.int32, (1, prefix_rows), 1)
    piece = sum((place >= at * part_rows).astype(jnp.int32) for at in range(1, 4))
    place = place - piece * part_rows
    token = sum((place >= at * pages).astype(jnp.int32) for at in range(1, 4))
    page = place - token * pages + seq_index * pages
    position = page * 16 + (own_part ^ piece) * 4 + token
    bias = jnp.where(position < limit, 0.0, HIDDEN).astype(jnp.float32)
    scale = LOG2E / math.sqrt(LANES)
    row = lax.broadcasted_iota(jnp.int32, (2 * tok_rows, tok_rows), 0) & (tok_rows - 1)
    column = lax.broadcasted_iota(jnp.int32, (2 * tok_rows, tok_rows), 1)
    stat_row = lax.broadcasted_iota(jnp.int32, (STAT_ROWS, tok_rows), 0)
    dims = (((1,), (1,)), ((), ()))
    for back, query_ref in enumerate(queries):
        group = (seq_index - back) & 3
        seen = row - column + (group - seq_index) * tok_rows >= 0
        query = jnp.concatenate([query_ref[:, :LANES], query_ref[:, LANES:]], axis=0)
        far = lax.dot_general(
            query, kv_ref[:prefix_rows, :LANES], dims, preferred_element_type=jnp.float32
        )
        near = lax.dot_general(
            query, kv_ref[prefix_rows:, :LANES], dims, preferred_element_type=jnp.float32
        )
        far = far * scale + bias
        near = jnp.where(seen, near * scale, HIDDEN)
        top = jnp.maximum(
            jnp.max(far, axis=1, keepdims=True), jnp.max(near, axis=1, keepdims=True)
        )
        top = jnp.maximum(top, FLOOR)
        far = jnp.exp2(far - top)
        near = jnp.exp2(near - top)
        total = jnp.sum(far, axis=1, keepdims=True) + jnp.sum(near, axis=1, keepdims=True)
        total = jnp.maximum(total, 1e-37)
        mixed = jnp.dot(
            far.astype(jnp.bfloat16),
            kv_ref[:prefix_rows, LANES:],
            preferred_element_type=jnp.float32,
        ) + jnp.dot(
            near.astype(jnp.bfloat16),
            kv_ref[prefix_rows:, LANES:],
            preferred_element_type=jnp.float32,
        )
        mixed = (mixed / total).astype(jnp.bfloat16)
        level = top + jnp.log2(total)
        stats = jnp.zeros((STAT_ROWS, tok_rows), jnp.float32)
        for head in range(2):
            rows = slice(head * tok_rows, (head + 1) * tok_rows)
            out_ref[group, :tok_rows, head * LANES : (head + 1) * LANES] = mixed[rows]
            turned = jnp.transpose(jnp.broadcast_to(level[rows], (tok_rows, LANES)))[:STAT_ROWS]
            high = turned.astype(jnp.bfloat16).astype(jnp.float32)
            middle = (turned - high).astype(jnp.bfloat16).astype(jnp.float32)
            low = turned - high - middle
            for at, value in enumerate((high, middle, low)):
                stats = jnp.where(stat_row == 3 * head + at, value, stats)
        out_ref[group, tok_rows:, :] = stats.astype(jnp.bfloat16)


def combine_kernel(part_ref, out_ref):
    groups = part_ref.shape[0]
    tok_rows = out_ref.shape[0]
    stats = [part_ref[group, tok_rows:, :].astype(jnp.float32) for group in range(groups)]
    shares = []
    for head in range(2):
        levels = [
            stat[3 * head : 3 * head + 1]
            + stat[3 * head + 1 : 3 * head + 2]
            + stat[3 * head + 2 : 3 * head + 3]
            for stat in stats
        ]
        top = functools.reduce(jnp.maximum, levels)
        weights = [jnp.exp2(level - top) for level in levels]
        total = functools.reduce(jnp.add, weights)
        shares.append([weight / total for weight in weights])
    share_row = lax.broadcasted_iota(jnp.int32, (LANES, tok_rows), 0)
    table = jnp.zeros((LANES, tok_rows), jnp.float32)
    for head in range(2):
        for group in range(groups):
            table = jnp.where(share_row == head * groups + group, shares[head][group], table)
    table = jnp.transpose(table)
    for head in range(2):
        lanes = slice(head * LANES, (head + 1) * LANES)
        mixed = jnp.zeros((tok_rows, LANES), jnp.float32)
        for group in range(groups):
            at = head * groups + group
            mixed = mixed + table[:, at : at + 1] * part_ref[group, :tok_rows, lanes].astype(
                jnp.float32
            )
        out_ref[:, lanes] = mixed


BLOCK = 16


def scan_tokens(step_ref, input_ref, bc_ref, decay, state, read_out):
    tokens = step_ref.shape[0]
    n_state = decay.shape[0]

    for half in range(tokens // LANES):
        bc_half = bc_ref[:, half * LANES : (half + 1) * LANES]

        def block(at, carried, half=half, bc_half=bc_half):
            start = pl.multiple_of(half * LANES + at * BLOCK, BLOCK)
            steps = step_ref[pl.ds(start, BLOCK), :]
            inputs = input_ref[pl.ds(start, BLOCK), :].astype(jnp.float32)
            drive = steps * inputs
            turned = pltpu.roll(bc_half, LANES - at * BLOCK, 1)
            rows = []
            for i in range(BLOCK):
                factor = jnp.exp2(steps[i : i + 1] * decay)
                carried = factor * carried + drive[i : i + 1] * turned[:n_state, i : i + 1]
                if read_out is not None:
                    term = carried * turned[n_state:, i : i + 1]
                    rows.append(jnp.sum(term, axis=0, keepdims=True))
            if read_out is not None:
                read_out(start, inputs, jnp.concatenate(rows, axis=0))
            return carried

        state = lax.fori_loop(0, LANES // BLOCK, block, state)
    return state


def local_scan_kernel(step_ref, input_ref, bc_ref, rate_ref, out_ref):
    decay = rate_ref[...] * (-LOG2E)
    n_state = decay.shape[0]
    out_ref[:n_state] = scan_tokens(
        step_ref, input_ref, bc_ref, decay, jnp.zeros(decay.shape, jnp.float32), None
    )
    total = jnp.sum(step_ref[...], axis=0, keepdims=True)
    out_ref[n_state:] = jnp.broadcast_to(total, (out_ref.shape[0] - n_state, total.shape[1]))


def full_scan_kernel(
    step_ref, input_ref, gate_ref, bc_ref, rate_ref, skip_ref, start_ref, *rest
):
    *carries, out_ref = rest
    decay = rate_ref[...] * (-LOG2E)
    n_state = decay.shape[0]
    state = start_ref[...]
    for back in range(len(carries), 0, -1):
        carry = carries[back - 1]
        factor = jnp.exp2(carry[n_state : n_state + 1, :] * decay)
        moved = factor * state + carry[:n_state, :]
        state = jnp.where(back <= lax.axis_index("seq"), moved, state)
    skip = skip_ref[...]

    def read_out(start, inputs, values):
        gate = gate_ref[pl.ds(start, BLOCK), :].astype(jnp.float32)
        out_ref[pl.ds(start, BLOCK), :] = (values + skip * inputs) * (gate / (1.0 + jnp.exp(-gate)))

    scan_tokens(step_ref, input_ref, bc_ref, decay, state, read_out)


def call(kernel, out, specs, args, mib, scratch=()):
    return pl.pallas_call(
        kernel,
        out_shape=out,
        in_specs=specs,
        out_specs=vmem(),
        scratch_shapes=list(scratch),
        compiler_params=params(mib),
    )(*args)


def shifted(value, axis, steps):
    count = lax.axis_size(axis)
    return lax.ppermute(value, axis, [(i, (i + steps) % count) for i in range(count)])


def from_all(value, axis):
    return [value] + [shifted(value, axis, steps) for steps in range(1, lax.axis_size(axis))]


def swapped(value, flip):
    count = lax.axis_size("mp")
    return lax.ppermute(value, "mp", [(source, source ^ flip) for source in range(count)])


def on_device(
    queries,
    span_kv,
    pool_kv,
    page_owner,
    page_slot,
    prefix_len,
    ssm_input,
    gate_z,
    time_step,
    bc_weight,
    decay_rate,
    skip_gain,
    state_pool,
    state_owner,
    state_slot,
):
    n_seq, n_mp, n_cache = (lax.axis_size(axis) for axis in ("seq", "mp", "cache"))
    seq_index, mp_index, request = (lax.axis_index(axis) for axis in ("seq", "mp", "cache"))
    tok_rows = queries.shape[1]
    kv_heads, width = span_kv.shape[2], span_kv.shape[3]
    pool_pages, page_len = pool_kv.shape[:2]
    pages_dev = page_owner.shape[1] // n_seq
    sharers = n_mp // kv_heads
    page_part = page_len // sharers

    quarter_owner = lax.dynamic_slice_in_dim(page_owner[:, :, 0], seq_index * pages_dev, pages_dev, 1)
    quarter_slot = lax.dynamic_slice_in_dim(page_slot, seq_index * pages_dev, pages_dev, 1)
    earlier = jnp.tril(jnp.ones((pages_dev, pages_dev), jnp.bool_), -1)
    same = quarter_owner[:, :, None] == quarter_owner[:, None, :]
    rank = jnp.sum((same & earlier).astype(jnp.int32), axis=2)
    mine = quarter_owner == mp_index * n_cache + request
    places = jnp.arange(2, dtype=jnp.int32)
    hit = mine[:, None, :] & (rank[:, None, :] == places[None, :, None])
    chosen = jnp.sum(jnp.where(hit, quarter_slot[:, None, :], 0), axis=2).reshape(-1)

    inputs = ssm_input[0]
    sums = lax.dot_general(
        bc_weight, inputs, (((0,), (1,)), ((), ())), preferred_element_type=jnp.float32
    )
    sums = jnp.broadcast_to(sums.astype(jnp.bfloat16)[None], (n_mp // 2,) + sums.shape)
    sums, pool_kv = lax.optimization_barrier((sums, pool_kv))
    chips = [[2 * chip + core for chip in range(n_mp // 2)] for core in range(2)]
    sums = lax.all_to_all(
        sums, "mp", split_axis=0, concat_axis=0, tiled=True, axis_index_groups=chips
    )
    outgoing = call(
        pack_kernel,
        jax.ShapeDtypeStruct((n_cache, n_mp * 2 * page_part, width), jnp.bfloat16),
        [smem(), vmem()],
        (chosen, pool_kv.reshape(pool_pages, page_len * kv_heads, width)),
        24,
    )

    outgoing, sums, queries, state_pool = lax.optimization_barrier(
        (outgoing, sums, queries, state_pool)
    )
    received = lax.all_to_all(
        outgoing.reshape(n_cache * n_mp, 2 * page_part, width),
        ("cache", "mp"),
        split_axis=0,
        concat_axis=0,
        tiled=True,
    ).reshape(n_cache * n_mp * 2 * page_part, width)
    bc = jnp.sum(sums.astype(jnp.float32), axis=0)
    bc = bc + swapped(bc, 1)

    rate = decay_rate.T
    state_shape = jax.ShapeDtypeStruct(rate.shape, jnp.float32)
    pair, crossing, near_state, span_tile = pl.pallas_call(
        prepare_kernel,
        out_shape=(
            jax.ShapeDtypeStruct((2,) + rate.shape, jnp.float32),
            state_shape,
            state_shape,
            jax.ShapeDtypeStruct((tok_rows, width), jnp.bfloat16),
        ),
        in_specs=[smem(), smem(), vmem(), vmem()],
        out_specs=(vmem(),) * 4,
        compiler_params=params(24),
    )(state_owner, state_slot, state_pool.transpose(0, 2, 1), span_kv.reshape(-1, width))
    pair = lax.ppermute(pair, "cache", [(i, i ^ 1) for i in range(n_cache)])
    crossing = crossing + pair[1]
    near_state = near_state + pair[0]
    all_queries = from_all(queries[0], "seq")
    start_state = near_state + lax.ppermute(crossing, "cache", [(i, i ^ 2) for i in range(n_cache)])

    rate = decay_rate.T
    n_state = rate.shape[0]
    carry = call(
        local_scan_kernel,
        jax.ShapeDtypeStruct((n_state + 8, rate.shape[1]), jnp.float32),
        [vmem()] * 4,
        (time_step[0], inputs, bc, rate),
        24,
    )
    last = shifted(carry, "seq", 1)
    decay = jnp.exp2(carry[n_state : n_state + 1] * (rate * (-LOG2E)))
    both = jnp.concatenate(
        [decay * last[:n_state] + carry[:n_state], last[n_state:] + carry[n_state:]], axis=0
    )
    carries = [last, shifted(jnp.where(seq_index > 0, both, carry), "seq", 2)]
    received, carries, start_state, bc, all_queries, span_tile = lax.optimization_barrier(
        (received, carries, start_state, bc, all_queries, span_tile)
    )
    base = ((quarter_owner % n_cache) * n_mp + quarter_owner // n_cache) * 2 + rank
    asked = jnp.arange(n_cache, dtype=jnp.int32)[:, None] == request
    base = jnp.sum(jnp.where(asked, base, 0), axis=0) * page_part
    tokens = jnp.arange(page_part, dtype=jnp.int32)
    target = (base[None, :] + tokens[:, None]).reshape(-1, 1)
    own = call(
        compact_kernel,
        jax.ShapeDtypeStruct((page_part * pages_dev, width), jnp.bfloat16),
        [vmem()] * 2,
        (target, received),
        24,
    )
    across = swapped(own, 2)
    pieces = [own, swapped(own, 1), across, swapped(across, 1)]
    partial = call(
        attention_kernel,
        jax.ShapeDtypeStruct((n_seq, tok_rows + STAT_ROWS, queries.shape[2]), jnp.bfloat16),
        [smem()] + [vmem()] * 9,
        (prefix_len, *all_queries, *pieces, span_tile),
        40,
        [pltpu.VMEM((sharers * page_part * pages_dev + tok_rows, width), jnp.bfloat16)],
    )
    partial, bc, carries = lax.optimization_barrier((partial, bc, carries))
    ssm_out = call(
        full_scan_kernel,
        jax.ShapeDtypeStruct(inputs.shape, jnp.float32),
        [vmem()] * (7 + len(carries)),
        (
            time_step[0],
            inputs,
            gate_z[0],
            bc,
            rate,
            skip_gain.reshape(1, -1),
            start_state,
            *carries,
        ),
        24,
    )
    gathered = lax.all_to_all(partial, "seq", split_axis=0, concat_axis=0, tiled=True)
    attn_out = call(
        combine_kernel,
        jax.ShapeDtypeStruct((tok_rows, queries.shape[2]), jnp.float32),
        [vmem()],
        (gathered,),
        24,
    )
    return (attn_out[None], ssm_out[None])


def solution(mesh):
    in_specs = (
        P("cache", "seq", "mp"),
        P("cache", "seq", None, None),
        P(("mp", "cache"), None, None, None),
        P(),
        P(),
        P(),
        P("cache", "seq", "mp"),
        P("cache", "seq", "mp"),
        P("cache", "seq", "mp"),
        P("mp", None),
        P("mp", None),
        P("mp"),
        P("cache", "mp", None),
        P(),
        P(),
    )
    out_specs = (P("cache", "seq", "mp"), P("cache", "seq", "mp"))
    return jax.shard_map(
        on_device, mesh=mesh, in_specs=in_specs, out_specs=out_specs, check_vma=False
    )
```

```python
import functools
import math

import jax
import jax.numpy as jnp
from jax import lax
from jax.experimental import pallas as pl
from jax.experimental.pallas import tpu as pltpu
from jax.sharding import PartitionSpec as P

LOG2E = math.log2(math.e)
HIDDEN = -1e30
FLOOR = -1e29
LANES = 128
STAT_ROWS = 16
MIB = 1 << 20


def params(mib):
    return pltpu.CompilerParams(vmem_limit_bytes=mib * MIB)


def smem():
    return pl.BlockSpec(memory_space=pltpu.SMEM)


def vmem():
    return pl.BlockSpec(memory_space=pltpu.VMEM)


def pack_kernel(chosen_ref, pool_ref, out_ref):
    rows = lax.broadcasted_iota(jnp.int32, (256, 256), 0)
    columns = lax.broadcasted_iota(jnp.int32, (256, 256), 1)
    token, slot, part, head = rows & 3, (rows >> 2) & 1, (rows >> 3) & 3, rows >> 5
    wanted = slot * 128 + (part * 4 + token) * 8 + head
    pick = (columns == wanted).astype(jnp.float32).astype(jnp.bfloat16)
    for request in range(out_ref.shape[0]):
        pages = jnp.concatenate(
            [pool_ref[chosen_ref[2 * request]], pool_ref[chosen_ref[2 * request + 1]]], axis=0
        )
        out_ref[request] = jnp.dot(pick, pages, preferred_element_type=jnp.float32).astype(
            jnp.bfloat16
        )


def compact_kernel(target_ref, received_ref, out_ref):
    count, width = out_ref.shape[0], received_ref.shape[0]
    columns = lax.broadcasted_iota(jnp.int32, (count, width), 1)
    pick = (columns == target_ref[...]).astype(jnp.float32).astype(jnp.bfloat16)
    out_ref[...] = jnp.dot(pick, received_ref[...], preferred_element_type=jnp.float32).astype(
        jnp.bfloat16
    )


def project_kernel(weight_ref, input_ref, out_ref):
    sums = lax.dot_general(
        weight_ref[...],
        input_ref[...],
        (((1,), (1,)), ((), ())),
        preferred_element_type=jnp.float32,
    ).astype(jnp.bfloat16)
    for chip in range(out_ref.shape[0]):
        out_ref[chip] = sums


def prepare_kernel(owner_ref, slot_ref, state_ref, span_ref, pair_ref, crossing_ref, near_ref, tile_ref):
    request = lax.axis_index("cache")

    def held(index):
        mine = owner_ref[index] == request
        return jnp.where(mine, state_ref[slot_ref[index]], 0.0)

    pair_ref[0] = held(request ^ 1)
    pair_ref[1] = held(request ^ 3)
    crossing_ref[...] = held(request ^ 2)
    near_ref[...] = held(request)
    tokens, heads = tile_ref.shape[0], span_ref.shape[0] // tile_ref.shape[0]
    head = lax.axis_index("mp") >> 2
    some = 32
    rows = lax.broadcasted_iota(jnp.int32, (some, some * heads), 0)
    columns = lax.broadcasted_iota(jnp.int32, (some, some * heads), 1)
    pick = (columns == rows * heads + head).astype(jnp.float32).astype(jnp.bfloat16)
    for at in range(tokens // some):
        block = span_ref[at * some * heads : (at + 1) * some * heads, :]
        tile_ref[at * some : (at + 1) * some, :] = jnp.dot(
            pick, block, preferred_element_type=jnp.float32
        ).astype(jnp.bfloat16)


def attention_kernel(
    prefix_ref, *refs
):
    *queries, piece0, piece1, piece2, piece3, span_ref, out_ref, kv_ref = refs
    part_rows = piece0.shape[0]
    prefix_rows = 4 * part_rows
    tok_rows = span_ref.shape[0]
    for at, piece in enumerate((piece0, piece1, piece2, piece3)):
        kv_ref[at * part_rows : (at + 1) * part_rows, :] = piece[...]
    kv_ref[prefix_rows:, :] = span_ref[...]
    seq_index, limit = lax.axis_index("seq"), prefix_ref[lax.axis_index("cache")]
    own_part = lax.axis_index("mp") & 3
    pages = part_rows // 4
    place = lax.broadcasted_iota(jnp.int32, (1, prefix_rows), 1)
    piece = sum((place >= at * part_rows).astype(jnp.int32) for at in range(1, 4))
    place = place - piece * part_rows
    token = sum((place >= at * pages).astype(jnp.int32) for at in range(1, 4))
    page = place - token * pages + seq_index * pages
    position = page * 16 + (own_part ^ piece) * 4 + token
    bias = jnp.where(position < limit, 0.0, HIDDEN).astype(jnp.float32)
    scale = LOG2E / math.sqrt(LANES)
    row = lax.broadcasted_iota(jnp.int32, (2 * tok_rows, tok_rows), 0) & (tok_rows - 1)
    column = lax.broadcasted_iota(jnp.int32, (2 * tok_rows, tok_rows), 1)
    stat_row = lax.broadcasted_iota(jnp.int32, (STAT_ROWS, tok_rows), 0)
    dims = (((1,), (1,)), ((), ()))
    for back, query_ref in enumerate(queries):
        group = (seq_index - back) & 3
        seen = row - column + (group - seq_index) * tok_rows >= 0
        query = jnp.concatenate([query_ref[:, :LANES], query_ref[:, LANES:]], axis=0)
        far = lax.dot_general(
            query, kv_ref[:prefix_rows, :LANES], dims, preferred_element_type=jnp.float32
        )
        near = lax.dot_general(
            query, kv_ref[prefix_rows:, :LANES], dims, preferred_element_type=jnp.float32
        )
        far = far * scale + bias
        near = jnp.where(seen, near * scale, HIDDEN)
        top = jnp.maximum(
            jnp.max(far, axis=1, keepdims=True), jnp.max(near, axis=1, keepdims=True)
        )
        top = jnp.maximum(top, FLOOR)
        far = jnp.exp2(far - top)
        near = jnp.exp2(near - top)
        total = jnp.sum(far, axis=1, keepdims=True) + jnp.sum(near, axis=1, keepdims=True)
        total = jnp.maximum(total, 1e-37)
        mixed = jnp.dot(
            far.astype(jnp.bfloat16),
            kv_ref[:prefix_rows, LANES:],
            preferred_element_type=jnp.float32,
        ) + jnp.dot(
            near.astype(jnp.bfloat16),
            kv_ref[prefix_rows:, LANES:],
            preferred_element_type=jnp.float32,
        )
        mixed = (mixed / total).astype(jnp.bfloat16)
        level = top + jnp.log2(total)
        stats = jnp.zeros((STAT_ROWS, tok_rows), jnp.float32)
        for head in range(2):
            rows = slice(head * tok_rows, (head + 1) * tok_rows)
            out_ref[group, :tok_rows, head * LANES : (head + 1) * LANES] = mixed[rows]
            turned = jnp.transpose(jnp.broadcast_to(level[rows], (tok_rows, LANES)))[:STAT_ROWS]
            high = turned.astype(jnp.bfloat16).astype(jnp.float32)
            middle = (turned - high).astype(jnp.bfloat16).astype(jnp.float32)
            low = turned - high - middle
            for at, value in enumerate((high, middle, low)):
                stats = jnp.where(stat_row == 3 * head + at, value, stats)
        out_ref[group, tok_rows:, :] = stats.astype(jnp.bfloat16)


def combine_kernel(part_ref, out_ref):
    groups = part_ref.shape[0]
    tok_rows = out_ref.shape[0]
    stats = [part_ref[group, tok_rows:, :].astype(jnp.float32) for group in range(groups)]
    shares = []
    for head in range(2):
        levels = [
            stat[3 * head : 3 * head + 1]
            + stat[3 * head + 1 : 3 * head + 2]
            + stat[3 * head + 2 : 3 * head + 3]
            for stat in stats
        ]
        top = functools.reduce(jnp.maximum, levels)
        weights = [jnp.exp2(level - top) for level in levels]
        total = functools.reduce(jnp.add, weights)
        shares.append([weight / total for weight in weights])
    share_row = lax.broadcasted_iota(jnp.int32, (LANES, tok_rows), 0)
    table = jnp.zeros((LANES, tok_rows), jnp.float32)
    for head in range(2):
        for group in range(groups):
            table = jnp.where(share_row == head * groups + group, shares[head][group], table)
    table = jnp.transpose(table)
    for head in range(2):
        lanes = slice(head * LANES, (head + 1) * LANES)
        mixed = jnp.zeros((tok_rows, LANES), jnp.float32)
        for group in range(groups):
            at = head * groups + group
            mixed = mixed + table[:, at : at + 1] * part_ref[group, :tok_rows, lanes].astype(
                jnp.float32
            )
        out_ref[:, lanes] = mixed


BLOCK = 16


def scan_tokens(step_ref, input_ref, bc_ref, decay, state, read_out):
    tokens = step_ref.shape[0]
    n_state = decay.shape[0]

    for half in range(tokens // LANES):
        bc_half = bc_ref[:, half * LANES : (half + 1) * LANES]

        def block(at, carried, half=half, bc_half=bc_half):
            start = pl.multiple_of(half * LANES + at * BLOCK, BLOCK)
            steps = step_ref[pl.ds(start, BLOCK), :]
            inputs = input_ref[pl.ds(start, BLOCK), :].astype(jnp.float32)
            drive = steps * inputs
            turned = pltpu.roll(bc_half, LANES - at * BLOCK, 1)
            rows = []
            for i in range(BLOCK):
                factor = jnp.exp2(steps[i : i + 1] * decay)
                carried = factor * carried + drive[i : i + 1] * turned[:n_state, i : i + 1]
                if read_out is not None:
                    term = carried * turned[n_state:, i : i + 1]
                    rows.append(jnp.sum(term, axis=0, keepdims=True))
            if read_out is not None:
                read_out(start, inputs, jnp.concatenate(rows, axis=0))
            return carried

        state = lax.fori_loop(0, LANES // BLOCK, block, state)
    return state


def local_scan_kernel(step_ref, input_ref, bc_ref, rate_ref, out_ref):
    decay = rate_ref[...] * (-LOG2E)
    n_state = decay.shape[0]
    out_ref[:n_state] = scan_tokens(
        step_ref, input_ref, bc_ref, decay, jnp.zeros(decay.shape, jnp.float32), None
    )
    total = jnp.sum(step_ref[...], axis=0, keepdims=True)
    out_ref[n_state:] = jnp.broadcast_to(total, (out_ref.shape[0] - n_state, total.shape[1]))


def full_scan_kernel(
    step_ref, input_ref, gate_ref, bc_ref, rate_ref, skip_ref, start_ref, *rest
):
    *carries, out_ref = rest
    decay = rate_ref[...] * (-LOG2E)
    n_state = decay.shape[0]
    state = start_ref[...]
    for back in range(len(carries), 0, -1):
        carry = carries[back - 1]
        factor = jnp.exp2(carry[n_state : n_state + 1, :] * decay)
        moved = factor * state + carry[:n_state, :]
        state = jnp.where(back <= lax.axis_index("seq"), moved, state)
    skip = skip_ref[...]

    def read_out(start, inputs, values):
        gate = gate_ref[pl.ds(start, BLOCK), :].astype(jnp.float32)
        out_ref[pl.ds(start, BLOCK), :] = (values + skip * inputs) * (gate / (1.0 + jnp.exp(-gate)))

    scan_tokens(step_ref, input_ref, bc_ref, decay, state, read_out)


def call(kernel, out, specs, args, mib, scratch=()):
    return pl.pallas_call(
        kernel,
        out_shape=out,
        in_specs=specs,
        out_specs=vmem(),
        scratch_shapes=list(scratch),
        compiler_params=params(mib),
    )(*args)


def shifted(value, axis, steps):
    count = lax.axis_size(axis)
    return lax.ppermute(value, axis, [(i, (i + steps) % count) for i in range(count)])


def from_all(value, axis):
    return [value] + [shifted(value, axis, steps) for steps in range(1, lax.axis_size(axis))]


def swapped(value, flip):
    count = lax.axis_size("mp")
    return lax.ppermute(value, "mp", [(source, source ^ flip) for source in range(count)])


def on_device(
    queries,
    span_kv,
    pool_kv,
    page_owner,
    page_slot,
    prefix_len,
    ssm_input,
    gate_z,
    time_step,
    bc_weight,
    decay_rate,
    skip_gain,
    state_pool,
    state_owner,
    state_slot,
):
    n_seq, n_mp, n_cache = (lax.axis_size(axis) for axis in ("seq", "mp", "cache"))
    seq_index, mp_index, request = (lax.axis_index(axis) for axis in ("seq", "mp", "cache"))
    tok_rows = queries.shape[1]
    kv_heads, width = span_kv.shape[2], span_kv.shape[3]
    pool_pages, page_len = pool_kv.shape[:2]
    pages_dev = page_owner.shape[1] // n_seq
    sharers = n_mp // kv_heads
    page_part = page_len // sharers

    quarter_owner = lax.dynamic_slice_in_dim(page_owner[:, :, 0], seq_index * pages_dev, pages_dev, 1)
    quarter_slot = lax.dynamic_slice_in_dim(page_slot, seq_index * pages_dev, pages_dev, 1)
    earlier = jnp.tril(jnp.ones((pages_dev, pages_dev), jnp.bool_), -1)
    same = quarter_owner[:, :, None] == quarter_owner[:, None, :]
    rank = jnp.sum((same & earlier).astype(jnp.int32), axis=2)
    mine = quarter_owner == mp_index * n_cache + request
    places = jnp.arange(2, dtype=jnp.int32)
    hit = mine[:, None, :] & (rank[:, None, :] == places[None, :, None])
    chosen = jnp.sum(jnp.where(hit, quarter_slot[:, None, :], 0), axis=2).reshape(-1)

    inputs = ssm_input[0]
    sums = call(
        project_kernel,
        jax.ShapeDtypeStruct((n_mp // 2, bc_weight.shape[1], tok_rows), jnp.bfloat16),
        [vmem()] * 2,
        (bc_weight.T, inputs),
        24,
    )
    sums, pool_kv = lax.optimization_barrier((sums, pool_kv))
    chips = [[2 * chip + core for chip in range(n_mp // 2)] for core in range(2)]
    sums = lax.all_to_all(
        sums, "mp", split_axis=0, concat_axis=0, tiled=True, axis_index_groups=chips
    )
    outgoing = call(
        pack_kernel,
        jax.ShapeDtypeStruct((n_cache, n_mp * 2 * page_part, width), jnp.bfloat16),
        [smem(), vmem()],
        (chosen, pool_kv.reshape(pool_pages, page_len * kv_heads, width)),
        24,
    )

    outgoing, sums, queries, state_pool = lax.optimization_barrier(
        (outgoing, sums, queries, state_pool)
    )
    received = lax.all_to_all(
        outgoing.reshape(n_cache * n_mp, 2 * page_part, width),
        ("cache", "mp"),
        split_axis=0,
        concat_axis=0,
        tiled=True,
    ).reshape(n_cache * n_mp * 2 * page_part, width)
    bc = jnp.sum(sums.astype(jnp.float32), axis=0)
    bc = bc + swapped(bc, 1)

    rate = decay_rate.T
    state_shape = jax.ShapeDtypeStruct(rate.shape, jnp.float32)
    pair, crossing, near_state, span_tile = pl.pallas_call(
        prepare_kernel,
        out_shape=(
            jax.ShapeDtypeStruct((2,) + rate.shape, jnp.float32),
            state_shape,
            state_shape,
            jax.ShapeDtypeStruct((tok_rows, width), jnp.bfloat16),
        ),
        in_specs=[smem(), smem(), vmem(), vmem()],
        out_specs=(vmem(),) * 4,
        compiler_params=params(24),
    )(state_owner, state_slot, state_pool.transpose(0, 2, 1), span_kv.reshape(-1, width))
    pair = lax.ppermute(pair, "cache", [(i, i ^ 1) for i in range(n_cache)])
    crossing = crossing + pair[1]
    near_state = near_state + pair[0]
    all_queries = from_all(queries[0], "seq")
    start_state = near_state + lax.ppermute(crossing, "cache", [(i, i ^ 2) for i in range(n_cache)])

    rate = decay_rate.T
    n_state = rate.shape[0]
    carry = call(
        local_scan_kernel,
        jax.ShapeDtypeStruct((n_state + 8, rate.shape[1]), jnp.float32),
        [vmem()] * 4,
        (time_step[0], inputs, bc, rate),
        24,
    )
    last = shifted(carry, "seq", 1)
    decay = jnp.exp2(carry[n_state : n_state + 1] * (rate * (-LOG2E)))
    both = jnp.concatenate(
        [decay * last[:n_state] + carry[:n_state], last[n_state:] + carry[n_state:]], axis=0
    )
    carries = [last, shifted(jnp.where(seq_index > 0, both, carry), "seq", 2)]
    received, carries, start_state, bc, all_queries, span_tile = lax.optimization_barrier(
        (received, carries, start_state, bc, all_queries, span_tile)
    )
    base = ((quarter_owner % n_cache) * n_mp + quarter_owner // n_cache) * 2 + rank
    asked = jnp.arange(n_cache, dtype=jnp.int32)[:, None] == request
    base = jnp.sum(jnp.where(asked, base, 0), axis=0) * page_part
    tokens = jnp.arange(page_part, dtype=jnp.int32)
    target = (base[None, :] + tokens[:, None]).reshape(-1, 1)
    own = call(
        compact_kernel,
        jax.ShapeDtypeStruct((page_part * pages_dev, width), jnp.bfloat16),
        [vmem()] * 2,
        (target, received),
        24,
    )
    across = swapped(own, 2)
    pieces = [own, swapped(own, 1), across, swapped(across, 1)]
    partial = call(
        attention_kernel,
        jax.ShapeDtypeStruct((n_seq, tok_rows + STAT_ROWS, queries.shape[2]), jnp.bfloat16),
        [smem()] + [vmem()] * 9,
        (prefix_len, *all_queries, *pieces, span_tile),
        40,
        [pltpu.VMEM((sharers * page_part * pages_dev + tok_rows, width), jnp.bfloat16)],
    )
    partial, bc, carries = lax.optimization_barrier((partial, bc, carries))
    ssm_out = call(
        full_scan_kernel,
        jax.ShapeDtypeStruct(inputs.shape, jnp.float32),
        [vmem()] * (7 + len(carries)),
        (
            time_step[0],
            inputs,
            gate_z[0],
            bc,
            rate,
            skip_gain.reshape(1, -1),
            start_state,
            *carries,
        ),
        24,
    )
    gathered = lax.all_to_all(partial, "seq", split_axis=0, concat_axis=0, tiled=True)
    attn_out = call(
        combine_kernel,
        jax.ShapeDtypeStruct((tok_rows, queries.shape[2]), jnp.float32),
        [vmem()],
        (gathered,),
        24,
    )
    return (attn_out[None], ssm_out[None])


def solution(mesh):
    in_specs = (
        P("cache", "seq", "mp"),
        P("cache", "seq", None, None),
        P(("mp", "cache"), None, None, None),
        P(),
        P(),
        P(),
        P("cache", "seq", "mp"),
        P("cache", "seq", "mp"),
        P("cache", "seq", "mp"),
        P("mp", None),
        P("mp", None),
        P("mp"),
        P("cache", "mp", None),
        P(),
        P(),
    )
    out_specs = (P("cache", "seq", "mp"), P("cache", "seq", "mp"))
    return jax.shard_map(
        on_device, mesh=mesh, in_specs=in_specs, out_specs=out_specs, check_vma=False
    )
```
